32 devices in a mesh: groups: 2 (over y), expert: 4 (over x, core), tensor: 4 (over z).
Axes of the slice: x: 2, y: 2, z: 4, core: 2. Of those that a mesh axis runs over, the one named last changes fastest.
Arguments:
- tokens: bfloat16 [1024, 3072], P(('groups', 'expert'), 'tensor'), parts along dimension 0, may hold values from -6 to 6
- teacher_routes: int32 [1024, 2], P(('groups', 'expert')), parts along dimension 0, may hold values from 0 to 3, all different within a row; in each aligned block of 128 rows (0 to 127, 128 to 255, ...) at most 80 rows name the same one
- teacher_share: float32 [1024], P(('groups', 'expert')), parts along dimension 0, may hold values from 0.1 to 0.9
- student_routes: int32 [1024, 1], P(('groups', 'expert')), parts along dimension 0, may hold values from 0 to 3; in each aligned block of 128 rows (0 to 127, 128 to 255, ...) at most 48 rows name the same one
- gate_weight: bfloat16 [4, 3072, 8192], P('expert', None, 'tensor'), may hold values from -0.109375 to 0.109375
- up_weight: bfloat16 [4, 3072, 8192], P('expert', None, 'tensor'), may hold values from -0.109375 to 0.109375
- down_weight: bfloat16 [4, 8192, 3072], P('expert', 'tensor'), may hold values from -0.0625 to 0.0625
- enc_weight: float32 [4, 3072, 4096], P('expert', 'tensor'), may hold values from -0.109375 to 0.109375
- enc_bias: float32 [4, 4096], P('expert'), may hold values from -3 to 3
- dec_weight: float32 [4, 4096, 3072], P('expert', None, 'tensor'), may hold values from -0.09375 to 0.09375
Outputs:
- enc_grad: float32 [8, 3072, 4096], P(('groups', 'expert'), 'tensor'), parts along dimension 0
- bias_grad: float32 [8, 4096], P(('groups', 'expert')), parts along dimension 0
- dec_grad: float32 [8, 4096, 3072], P(('groups', 'expert'), None, 'tensor'), parts along dimension 0
The draws below stay inside these ranges and needn't reach their ends.
There are 2 independent parts, one for each index of `groups`. The reference program is written for one: setup_inputs(seed, part) draws one part's arguments, and reference() takes and returns one part's arrays. A program takes and returns all parts, laid end to end along the dimension named above; an argument that names none is the same for every part. Nothing has to cross between parts.
Inputs may be any that keep to these rules, and one draw needn't show every extreme that they name: `teacher_routes`: each row names two different experts. In each aligned block of 128 rows (the tokens of one index of expert) no expert is named more than 80 times, and in some blocks one is named exactly 80 times. `student_routes`: in each aligned block of 128 rows no dictionary is named more than 48 times, and in some blocks one is named exactly 48 times.
All inputs are finite; a program needn't handle non-finite values.
Results may differ from the reference program's by a relative error of at most 0.005.
Values may be sent and summed in bfloat16 or wider, within the bound.
A program may use at most 192 MiB of HBM per device.

```python
import math
import jax
import jax.numpy as jnp
import numpy as np
from jax import lax

D = 3072
FF = 8192
EXPERTS = 4
LAT = 4096
DICTS = 4
TOK_DEV = 128
CAP = 80
CAP_S = 48
SPAN = 1
TOKENS = 512
N_EXPERT = 4
N_TENSOR = 4


def level_of(rng, dims, cuts, smallest, top_value):
    factor_of = 1.0
    for dim, parts in cuts:
        steps = jax.random.uniform(jax.random.fold_in(jax.random.fold_in(rng, 6), dim), (parts,), jnp.float32, smallest / len(cuts), top_value / len(cuts))
        factor_of = factor_of * jnp.repeat(jnp.exp(steps), dims[dim] // parts).reshape((-1,) + (1,) * (len(dims) - 1 - dim))
    return factor_of


def routed_block(key, own, number, rows, number_of, top, bound, slope):
    ranking = jax.random.permutation(key, number_of)
    packed, usual = load_shares(number_of, rows * top, bound, slope, True), load_shares(number_of, rows * top, bound, slope, False)
    places = jnp.arange(number_of)

    def named(tallies, rotation):
        used = int((tallies > 0).sum())
        fixed = max(1, used // 4)
        passed = fixed + (places - fixed + rotation * (used - fixed)) % max(1, number_of - fixed)
        return jnp.zeros((number_of,), jnp.int32).at[ranking[jnp.where(places < fixed, places, passed)]].set(jnp.asarray(tallies, jnp.int32))

    tallies = jnp.where(number % 4 == 0, named(packed, number // 4), named(usual, number - number // 4 - 1))
    mixed = jax.random.permutation(jax.random.fold_in(own, 3), number_of)
    source_of, receiver = mixed[0:number_of // 2 * 2:2], mixed[1:number_of // 2 * 2:2]
    slack = jnp.minimum(tallies[source_of] - 1, bound - tallies[receiver]) // 2
    slack = jnp.where((source_of == ranking[0]) | (receiver == ranking[0]) | (tallies[receiver] == 0), 0, jnp.maximum(slack, 0))
    passed = jax.random.randint(jax.random.fold_in(own, 4), (number_of // 2,), 0, 1 << 20) % (slack + 1)
    tallies = tallies.at[source_of].add(-passed).at[receiver].add(passed)
    items = jnp.searchsorted(jnp.cumsum(tallies), jnp.arange(rows * top), side="right").astype(jnp.int32)
    grid = items.reshape(top, rows).T
    grid = grid[jax.random.permutation(jax.random.fold_in(own, 1), rows)]
    rotation = jax.random.randint(jax.random.fold_in(own, 2), (rows, 1), 0, top)
    return jnp.take_along_axis(grid, (jnp.arange(top)[None, :] + rotation) % top, axis=1)


def load_shares(amount, total, reach, lean, full):
    portions = [(1 << 20) // math.isqrt(grade ** lean) + 1 for grade in range(1, amount + 1)]
    largest = reach if full else min(reach, max(-(-total // amount), total * portions[0] // sum(portions)))
    least = 1 if total - largest >= amount - 1 else 0
    given, surplus = [largest] + [least] * (amount - 1), total - largest - least * (amount - 1)
    while surplus > 0:
        free = [i for i in range(1, amount) if given[i] < largest] or [i for i in range(1, amount) if given[i] < reach]
        whole, left = sum([portions[i] for i in free]), surplus
        for i in free:
            extra = min(reach - given[i], max(1, left * portions[i] // whole), surplus)
            given[i] = given[i] + extra
            surplus = surplus - extra
    return np.array(given)


def gaussian(stream_key, dims, deviation, most, split=(), kind=jnp.bfloat16):
    loudness = level_of(stream_key, dims, split, -0.22, 0.18) if split else 1.0
    result = jax.random.normal(stream_key, dims, jnp.float32) * deviation * loudness
    return jnp.minimum(jnp.maximum(result, -most), most).astype(kind)


def setup_inputs(seed: int = 0, part: int = 0) -> dict:
    streams_of = jax.random.split(jax.random.key(seed), 11)
    part_splits = jax.random.split(jax.random.fold_in(streams_of[10], part), 11)
    tokens = gaussian(part_splits[0], (TOKENS, D), 1.0, 6.0, ((0, 4), (1, 4)))
    teacher_routes_keys = jax.random.split(jax.random.fold_in(part_splits[1], 1), TOKENS // TOK_DEV)
    teacher_routes_turns = jax.random.permutation(jax.random.fold_in(part_splits[1], 3), TOKENS // TOK_DEV)
    teacher_routes = jax.vmap(lambda own, number: routed_block(jax.random.fold_in(part_splits[1], 2), own, number, TOK_DEV, EXPERTS, 2, CAP, 1))(teacher_routes_keys, teacher_routes_turns).reshape((TOKENS, 2))
    teacher_share = jnp.clip(0.1 + 0.79999997 * jax.random.uniform(part_splits[2], (TOKENS,), jnp.float32) ** level_of(part_splits[2], (TOKENS,), ((0, 4),), -0.2, 0.2), 0.1, 0.9)
    student_routes_keys = jax.random.split(jax.random.fold_in(part_splits[3], 1), TOKENS // TOK_DEV)
    student_routes_turns = jax.random.permutation(jax.random.fold_in(part_splits[3], 3), TOKENS // TOK_DEV)
    student_routes = jax.vmap(lambda own, number: routed_block(jax.random.fold_in(part_splits[3], 2), own, number, TOK_DEV, DICTS, 1, CAP_S, 2))(student_routes_keys, student_routes_turns).reshape((TOKENS, 1))
    gate_weight = gaussian(streams_of[4], (EXPERTS * SPAN, D, FF // SPAN), D ** -0.5, 0.109375, ((0, 4), (2, 4)))
    up_weight = gaussian(streams_of[5], (EXPERTS * SPAN, D, FF // SPAN), D ** -0.5, 0.109375, ((0, 4), (2, 4)))
    down_weight = gaussian(streams_of[6], (EXPERTS * SPAN, FF // SPAN, D), FF ** -0.5, 0.0625, ((0, 4), (1, 4)))
    enc_weight = gaussian(streams_of[7], (DICTS * SPAN, D, LAT // SPAN), D ** -0.5, 0.109375, ((0, 4), (1, 4)), jnp.float32)
    enc_bias = gaussian(streams_of[8], (DICTS * SPAN, LAT // SPAN), 0.5, 3.0, ((0, 4),), jnp.float32)
    dec_weight = gaussian(streams_of[9], (DICTS * SPAN, LAT // SPAN, D), LAT ** -0.5, 0.09375, ((0, 4), (2, 4)), jnp.float32)
    return dict(tokens=tokens, teacher_routes=teacher_routes, teacher_share=teacher_share, student_routes=student_routes, gate_weight=gate_weight, up_weight=up_weight, down_weight=down_weight, enc_weight=enc_weight, enc_bias=enc_bias, dec_weight=dec_weight)


error_scale = 0.0625

def activation(values):
    return jax.nn.gelu(values, approximate=True)

def slot_index(routes, group_count, capacity):
    pick_count = routes.shape[1]
    blocks = routes.reshape(N_EXPERT, TOK_DEV * pick_count)
    onehot = (blocks[:, :, None] == jnp.arange(group_count, dtype=jnp.int32)[None, None, :]).astype(jnp.int32)
    before = jnp.cumsum(onehot, axis=1) - onehot
    position = lax.optimization_barrier(jnp.sum(before * onehot, axis=2))
    device_base = (jnp.arange(N_EXPERT, dtype=jnp.int32) * capacity)[:, None]
    return (position + device_base).astype(jnp.int32).reshape(TOK_DEV * N_EXPERT, pick_count)

def fill_rows(source, slot_ids, hit_mask, row_total):
    where_row = jnp.where(hit_mask, slot_ids, row_total).astype(jnp.int32)
    buffer = jnp.zeros((row_total + 1, source.shape[1]), source.dtype)
    for pick_id in range(slot_ids.shape[1]):
        buffer = buffer.at[where_row[:, pick_id]].set(source)
    return buffer[:row_total]

def reference(tokens, teacher_routes, teacher_share, student_routes, gate_weight, up_weight, down_weight, enc_weight, enc_bias, dec_weight):
    row_total = N_EXPERT * CAP
    stretch_size = FF // SPAN // N_TENSOR
    teacher_slots = slot_index(teacher_routes, EXPERTS, CAP)
    tables = []
    for expert_id in range(EXPERTS):
        buffer = fill_rows(tokens, teacher_slots, teacher_routes == expert_id, row_total)
        running = jnp.zeros((row_total, D), jnp.float32)
        for span_id in range(SPAN):
            member = expert_id * SPAN + span_id
            gate_proj = jnp.dot(buffer, gate_weight[member], preferred_element_type=jnp.float32)
            up_proj = jnp.dot(buffer, up_weight[member], preferred_element_type=jnp.float32)
            hidden = (jax.nn.silu(gate_proj) * up_proj).astype(jnp.bfloat16)
            pieces = jnp.einsum('rtc,tcd->trd', hidden.reshape(row_total, N_TENSOR, stretch_size).astype(jnp.float32), down_weight[member].reshape(N_TENSOR, stretch_size, D).astype(jnp.float32))
            pieces = lax.optimization_barrier(pieces.astype(jnp.bfloat16)).astype(jnp.float32)
            expert_part = lax.optimization_barrier(lax.optimization_barrier(jnp.sum(pieces, axis=0)).astype(jnp.bfloat16))
            running = running + expert_part.astype(jnp.float32)
        tables.append(running)
    table = jnp.stack(tables)
    first_row = table[teacher_routes[:, 0], teacher_slots[:, 0]]
    second_row = table[teacher_routes[:, 1], teacher_slots[:, 1]]
    share_col = teacher_share[:, None]
    target = share_col * first_row + (1.0 - share_col) * second_row
    slot_total = N_EXPERT * CAP_S
    student_slots = slot_index(student_routes, DICTS, CAP_S)
    predicted = jnp.zeros((TOK_DEV * N_EXPERT, D), jnp.float32)
    saved_inputs = []
    saved_pre = []
    for dict_id in range(DICTS):
        hit_mask = student_routes == dict_id
        inputs = fill_rows(tokens, student_slots, hit_mask, slot_total).astype(jnp.float32)
        estimate = jnp.zeros((slot_total, D), jnp.float32)
        pre_list = []
        for span_id in range(SPAN):
            member = dict_id * SPAN + span_id
            pre = jnp.dot(inputs, enc_weight[member], precision=lax.Precision.HIGHEST, preferred_element_type=jnp.float32) + enc_bias[member][None, :]
            latent = activation(pre)
            estimate = estimate + jnp.dot(latent, dec_weight[member], precision=lax.Precision.HIGHEST, preferred_element_type=jnp.float32)
            pre_list.append(pre)
        chosen = estimate[student_slots[:, 0]]
        predicted = predicted + jnp.where(hit_mask[:, 0][:, None], chosen, 0.0)
        saved_inputs.append(inputs)
        saved_pre.append(pre_list)
    error = (predicted - target) * error_scale
    enc_grads = []
    bias_grads = []
    dec_grads = []
    for dict_id in range(DICTS):
        hit_mask = student_routes == dict_id
        error_rows = fill_rows(error, student_slots, hit_mask, slot_total)
        inputs = saved_inputs[dict_id]
        for span_id in range(SPAN):
            member = dict_id * SPAN + span_id
            latent, gelu_back = jax.vjp(activation, saved_pre[dict_id][span_id])
            dec_grads.append(jnp.dot(latent.T, error_rows, precision=lax.Precision.HIGHEST, preferred_element_type=jnp.float32))
            latent_grad = jnp.dot(error_rows, dec_weight[member].T, precision=lax.Precision.HIGHEST, preferred_element_type=jnp.float32)
            pre_grad = gelu_back(latent_grad)[0]
            enc_grads.append(jnp.dot(inputs.T, pre_grad, precision=lax.Precision.HIGHEST, preferred_element_type=jnp.float32))
            bias_grads.append(lax.optimization_barrier(jnp.sum(pre_grad, axis=0)))
    return (jnp.stack(enc_grads), jnp.stack(bias_grads), jnp.stack(dec_grads))
```

```python
import jax
import jax.numpy as jnp
from jax import lax
from jax.sharding import PartitionSpec as P

EXPERTS = 4
DICTS = 4
CAP = 80
CAP_S = 48


error_scale = 0.0625


def activation(values):
    return jax.nn.gelu(values, approximate=True)


def slot_table(routes, group_count, capacity):
    length, pick_count = routes.shape
    flat_ids = routes.reshape(length * pick_count)
    onehot = (flat_ids[:, None] == jnp.arange(group_count, dtype=jnp.int32)[None, :]).astype(
        jnp.int32
    )
    before = jnp.cumsum(onehot, axis=0) - onehot
    position = jnp.sum(before * onehot, axis=1)
    return (flat_ids * capacity + position).reshape(length, pick_count)


def on_device(
    tokens,
    teacher_routes,
    teacher_share,
    student_routes,
    gate_weight,
    up_weight,
    down_weight,
    enc_weight,
    enc_bias,
    dec_weight,
):
    span_size = lax.axis_size("expert") // EXPERTS
    col_width = tokens.shape[1]
    full_width = col_width * lax.axis_size("tensor")
    teacher_slot = slot_table(teacher_routes, EXPERTS, CAP)
    slot_hits = (
        teacher_slot[:, :, None] == jnp.arange(EXPERTS * CAP, dtype=jnp.int32)[None, None, :]
    )
    spread = jnp.any(slot_hits, axis=1).astype(jnp.bfloat16)
    shares = jnp.stack([teacher_share, 1.0 - teacher_share], axis=1)
    weighting = jnp.sum(jnp.where(slot_hits, shares[:, :, None], 0.0), axis=1)
    full_tokens = lax.all_gather(tokens, "tensor", axis=1, tiled=True)
    packed = jnp.einsum(
        "tc,tw->cw", spread, full_tokens, preferred_element_type=jnp.float32
    ).astype(jnp.bfloat16)
    packed = packed.reshape(EXPERTS, CAP, full_tokens.shape[1])
    arrived = lax.all_to_all(
        jnp.repeat(packed, span_size, axis=0), "expert", split_axis=0, concat_axis=0, tiled=True
    )
    sources, slot_count, _ = arrived.shape
    flat_rows = arrived.reshape(sources * slot_count, full_width)
    gate_proj = jnp.dot(flat_rows, gate_weight[0], preferred_element_type=jnp.float32)
    up_proj = jnp.dot(flat_rows, up_weight[0], preferred_element_type=jnp.float32)
    hidden = (jax.nn.silu(gate_proj) * up_proj).astype(jnp.bfloat16)
    part_rows = jnp.dot(hidden, down_weight[0], preferred_element_type=jnp.float32)
    part_rows = part_rows.astype(jnp.bfloat16).reshape(sources, slot_count, full_width)
    returned = lax.all_to_all(part_rows, "expert", split_axis=0, concat_axis=0, tiled=True)
    summed = jnp.sum(
        returned.astype(jnp.float32).reshape(EXPERTS, span_size, CAP, full_width), axis=1
    ).reshape(EXPERTS * CAP, full_width)
    mixed = jnp.dot(
        weighting, summed, precision=lax.Precision.HIGH, preferred_element_type=jnp.float32
    ).astype(jnp.bfloat16)
    tensor_size = lax.axis_size("tensor")
    token_count = mixed.shape[0]
    mixed = mixed.reshape(token_count, tensor_size, col_width).transpose(1, 0, 2)
    target = (
        lax.psum_scatter(mixed, "tensor", scatter_dimension=0, tiled=True)
        .reshape(token_count, col_width)
        .astype(jnp.float32)
    )
    student_slot = slot_table(student_routes, DICTS, CAP_S)
    picked = student_slot[:, 0][:, None] == jnp.arange(DICTS * CAP_S, dtype=jnp.int32)[None, :]
    sending = picked.astype(jnp.bfloat16)
    selector = picked.astype(jnp.float32)
    outgoing = jnp.einsum("tc,tw->cw", sending, tokens, preferred_element_type=jnp.float32).astype(
        jnp.bfloat16
    )
    outgoing = jnp.repeat(outgoing.reshape(DICTS, CAP_S, col_width), span_size, axis=0)
    student_in = lax.all_to_all(outgoing, "expert", split_axis=0, concat_axis=0, tiled=True)
    sources = student_in.shape[0]
    rows = sources * CAP_S
    inputs_flat = student_in.reshape(rows, col_width)
    pre_part = jnp.dot(
        inputs_flat.astype(jnp.float32),
        enc_weight[0],
        precision=lax.Precision.HIGH,
        preferred_element_type=jnp.float32,
    )
    lat_size = pre_part.shape[1]
    lat_cols = lat_size // tensor_size

    def scatter_latents(part):
        blocks = part.reshape(rows, tensor_size, lat_cols).transpose(1, 0, 2)
        own = lax.psum_scatter(blocks, "tensor", scatter_dimension=0, tiled=True)
        return own.reshape(rows, lat_cols)

    def gather_latents(own):
        blocks = lax.all_gather(own.astype(jnp.bfloat16), "tensor", axis=0, tiled=False)
        return blocks.transpose(1, 0, 2).reshape(rows, lat_size)

    bias_own = lax.dynamic_slice_in_dim(
        enc_bias[0], lax.axis_index("tensor") * lat_cols, lat_cols
    )
    pre_own = scatter_latents(pre_part) + bias_own[None, :]
    latent_own, gelu_back = jax.vjp(activation, pre_own)
    latent = gather_latents(latent_own)
    partial_out = jnp.dot(
        latent,
        dec_weight[0].astype(jnp.bfloat16),
        preferred_element_type=jnp.float32,
    )
    back_parts = lax.all_to_all(
        partial_out.reshape(sources, CAP_S, col_width),
        "expert",
        split_axis=0,
        concat_axis=0,
        tiled=True,
    )
    estimate = jnp.sum(back_parts.reshape(DICTS, span_size, CAP_S, col_width), axis=1).reshape(
        DICTS * CAP_S, col_width
    )
    predicted = jnp.dot(
        selector, estimate, precision=lax.Precision.HIGHEST, preferred_element_type=jnp.float32
    )
    error_rows = (predicted - target) * error_scale
    error_slots = lax.dot_general(
        selector,
        error_rows,
        (((0,), (0,)), ((), ())),
        precision=lax.Precision.HIGHEST,
        preferred_element_type=jnp.float32,
    )
    error_slots = jnp.repeat(error_slots.reshape(DICTS, CAP_S, col_width), span_size, axis=0)
    error_back = lax.all_to_all(error_slots, "expert", split_axis=0, concat_axis=0, tiled=True)
    error_flat = error_back.reshape(rows, col_width)
    latent_part = lax.dot_general(
        error_flat,
        dec_weight[0],
        (((1,), (1,)), ((), ())),
        precision=lax.Precision.HIGH,
        preferred_element_type=jnp.float32,
    )
    latent_sum = scatter_latents(latent_part)
    dec_grad = lax.dot_general(
        latent,
        error_flat.astype(jnp.bfloat16),
        (((0,), (0,)), ((), ())),
        preferred_element_type=jnp.float32,
    )
    pre_grad = gather_latents(gelu_back(latent_sum)[0])
    enc_grad = lax.dot_general(
        inputs_flat,
        pre_grad,
        (((0,), (0,)), ((), ())),
        preferred_element_type=jnp.float32,
    )
    bias_grad = jnp.sum(pre_grad.astype(jnp.float32), axis=0)
    return (enc_grad[None], bias_grad[None], dec_grad[None])


def solution(mesh):
    return jax.shard_map(
        on_device,
        mesh=mesh,
        in_specs=(
            P(("groups", "expert"), "tensor"),
            P(("groups", "expert"), None),
            P(("groups", "expert")),
            P(("groups", "expert"), None),
            P("expert", None, "tensor"),
            P("expert", None, "tensor"),
            P("expert", "tensor", None),
            P("expert", "tensor", None),
            P("expert", None),
            P("expert", None, "tensor"),
        ),
        out_specs=(
            P(("groups", "expert"), "tensor", None),
            P(("groups", "expert"), None),
            P(("groups", "expert"), None, "tensor"),
        ),
        check_vma=False,
    )
```

```python
import functools
import math

import jax
import jax.numpy as jnp
from jax import lax
from jax.experimental import pallas as pl
from jax.experimental.pallas import tpu as pltpu
from jax.sharding import PartitionSpec as P

EXPERTS = 4
DICTS = 4
CAP = 80
CAP_S = 48


error_scale = 0.0625


PIECES = 4
BLOCK = 16
ROOT = math.sqrt(2.0 / math.pi)
MESH_IDS = pl.DeviceIdType.MESH


def gelu_tail(v):
    return jnp.tanh(ROOT * (v + 0.044715 * (v * v * v)))


def exchange_kernel(
    n, backward, part_ref, aux_ref, out_ref, *rest
):
    if backward:
        own_ref = None
        send32, recv32, send16, recv16, s32, r32, s16, r16, sg, rg = rest
    else:
        own_ref, send32, recv32, send16, recv16, s32, r32, s16, r16, sg, rg = rest
    rows, cols = recv32.shape
    piece = rows // PIECES
    me = lax.axis_index("tensor")
    pair, bit = me // 2, me % 2
    partner = 2 * pair + 1 - bit
    others = []
    for q in range(1, n // 2):
        for c in range(2):
            others.append(2 * ((pair + q) % (n // 2)) + c)

    def columns(index):
        return pl.ds(pl.multiple_of(index * cols, cols), cols)

    barrier = pltpu.get_barrier_semaphore()
    for peer in [partner] + others:
        pl.semaphore_signal(barrier, inc=1, device_id={"tensor": peer}, device_id_type=MESH_IDS)
    pl.semaphore_wait(barrier, n - 1)

    sends = []
    for h in range(PIECES):
        span = pl.ds(h * piece, piece)
        for i, peer in enumerate(others):

            @pl.loop(0, piece // BLOCK)
            def _(j):
                r = pl.ds(pl.multiple_of(h * piece + j * BLOCK, BLOCK), BLOCK)
                send16[i, r, :] = part_ref[r, columns(peer)].astype(jnp.bfloat16)

            copy = pltpu.make_async_remote_copy(
                src_ref=send16.at[i, span],
                dst_ref=recv16.at[me, span],
                send_sem=s16.at[h, i],
                recv_sem=r16.at[h, me],
                device_id={"tensor": peer},
                device_id_type=MESH_IDS,
            )
            copy.start()
            sends.append(copy)

        @pl.loop(0, piece // BLOCK)
        def _(j):
            r = pl.ds(pl.multiple_of(h * piece + j * BLOCK, BLOCK), BLOCK)
            send32[r, :] = part_ref[r, columns(partner)]

        copy = pltpu.make_async_remote_copy(
            src_ref=send32.at[span],
            dst_ref=recv32.at[span],
            send_sem=s32.at[h],
            recv_sem=r32.at[h],
            device_id={"tensor": partner},
            device_id_type=MESH_IDS,
        )
        copy.start()
        sends.append(copy)

    def arrival(ref, sem, peer):
        return pltpu.make_async_remote_copy(
            src_ref=ref,
            dst_ref=ref,
            send_sem=sem,
            recv_sem=sem,
            device_id={"tensor": peer},
            device_id_type=MESH_IDS,
        )

    for h in range(PIECES):
        span = pl.ds(h * piece, piece)
        arrival(recv32.at[span], r32.at[h], partner).wait_recv()
        for peer in others:
            arrival(recv16.at[peer, span], r16.at[h, peer], peer).wait_recv()

        @pl.loop(0, piece // BLOCK)
        def _(j):
            r = pl.ds(pl.multiple_of(h * piece + j * BLOCK, BLOCK), BLOCK)
            total = part_ref[r, columns(me)] + recv32[r, :]
            for peer in others:
                total = total + recv16[peer, r, :].astype(jnp.float32)
            if backward:
                v = aux_ref[r, :]
                t = gelu_tail(v)
                slope = 0.5 * (1.0 + t) + (0.5 * ROOT) * v * (1.0 - t * t) * (
                    1.0 + (3.0 * 0.044715) * (v * v)
                )
                value = total * slope
            else:
                v = total + aux_ref[:, columns(me)]
                own_ref[r, :] = v
                value = 0.5 * v * (1.0 + gelu_tail(v))
            out_ref[r, columns(me)] = value.astype(jnp.bfloat16)

        for i, peer in enumerate([partner] + others):
            copy = pltpu.make_async_remote_copy(
                src_ref=out_ref.at[span, columns(me)],
                dst_ref=out_ref.at[span, columns(me)],
                send_sem=sg.at[h, i],
                recv_sem=rg.at[h, me],
                device_id={"tensor": peer},
                device_id_type=MESH_IDS,
            )
            copy.start()
            sends.append(copy)

    for h in range(PIECES):
        span = pl.ds(h * piece, piece)
        for peer in [partner] + others:
            arrival(out_ref.at[span, columns(peer)], rg.at[h, peer], peer).wait_recv()
    for copy in sends:
        copy.wait_send()


def exchange(part, aux, backward):
    n = lax.axis_size("tensor")
    rows, width = part.shape
    cols = width // n
    vmem = pl.BlockSpec(memory_space=pltpu.VMEM)
    gathered = jax.ShapeDtypeStruct((rows, width), jnp.bfloat16)
    own = jax.ShapeDtypeStruct((rows, cols), jnp.float32)
    dma = pltpu.SemaphoreType.DMA
    return pl.pallas_call(
        functools.partial(exchange_kernel, n, backward),
        out_shape=gathered if backward else (gathered, own),
        in_specs=[vmem, vmem],
        out_specs=vmem if backward else (vmem, vmem),
        scratch_shapes=[
            pltpu.VMEM((rows, cols), jnp.float32),
            pltpu.VMEM((rows, cols), jnp.float32),
            pltpu.VMEM((n - 2, rows, cols), jnp.bfloat16),
            pltpu.VMEM((n, rows, cols), jnp.bfloat16),
            dma((PIECES,)),
            dma((PIECES,)),
            dma((PIECES, n - 2)),
            dma((PIECES, n)),
            dma((PIECES, n - 1)),
            dma((PIECES, n)),
        ],
        compiler_params=pltpu.CompilerParams(
            collective_id=1 if backward else 0,
            has_side_effects=True,
            vmem_limit_bytes=32 * 1024 * 1024,
        ),
        cost_estimate=pl.CostEstimate(
            flops=20 * rows * cols, bytes_accessed=rows * width * 6, transcendentals=rows * cols
        ),
    )(part, aux)


def slot_table(routes, group_count, capacity):
    length, pick_count = routes.shape
    flat_ids = routes.reshape(length * pick_count)
    onehot = (flat_ids[:, None] == jnp.arange(group_count, dtype=jnp.int32)[None, :]).astype(
        jnp.int32
    )
    before = jnp.cumsum(onehot, axis=0) - onehot
    position = jnp.sum(before * onehot, axis=1)
    return (flat_ids * capacity + position).reshape(length, pick_count)


def on_device(
    tokens,
    teacher_routes,
    teacher_share,
    student_routes,
    gate_weight,
    up_weight,
    down_weight,
    enc_weight,
    enc_bias,
    dec_weight,
):
    span_size = lax.axis_size("expert") // EXPERTS
    col_width = tokens.shape[1]
    full_width = col_width * lax.axis_size("tensor")
    teacher_slot = slot_table(teacher_routes, EXPERTS, CAP)
    slot_hits = (
        teacher_slot[:, :, None] == jnp.arange(EXPERTS * CAP, dtype=jnp.int32)[None, None, :]
    )
    spread = jnp.any(slot_hits, axis=1).astype(jnp.bfloat16)
    shares = jnp.stack([teacher_share, 1.0 - teacher_share], axis=1)
    weighting = jnp.sum(jnp.where(slot_hits, shares[:, :, None], 0.0), axis=1)
    full_tokens = lax.all_gather(tokens, "tensor", axis=1, tiled=True)
    packed = jnp.einsum(
        "tc,tw->cw", spread, full_tokens, preferred_element_type=jnp.float32
    ).astype(jnp.bfloat16)
    packed = packed.reshape(EXPERTS, CAP, full_tokens.shape[1])
    arrived = lax.all_to_all(
        jnp.repeat(packed, span_size, axis=0), "expert", split_axis=0, concat_axis=0, tiled=True
    )
    sources, slot_count, _ = arrived.shape
    flat_rows = arrived.reshape(sources * slot_count, full_width)
    gate_proj = jnp.dot(flat_rows, gate_weight[0], preferred_element_type=jnp.float32)
    up_proj = jnp.dot(flat_rows, up_weight[0], preferred_element_type=jnp.float32)
    hidden = (jax.nn.silu(gate_proj) * up_proj).astype(jnp.bfloat16)
    part_rows = jnp.dot(hidden, down_weight[0], preferred_element_type=jnp.float32)
    part_rows = part_rows.astype(jnp.bfloat16).reshape(sources, slot_count, full_width)
    returned = lax.all_to_all(part_rows, "expert", split_axis=0, concat_axis=0, tiled=True)
    summed = jnp.sum(
        returned.astype(jnp.float32).reshape(EXPERTS, span_size, CAP, full_width), axis=1
    ).reshape(EXPERTS * CAP, full_width)
    mixed = jnp.dot(
        weighting, summed, precision=lax.Precision.HIGH, preferred_element_type=jnp.float32
    ).astype(jnp.bfloat16)
    tensor_size = lax.axis_size("tensor")
    token_count = mixed.shape[0]
    mixed = mixed.reshape(token_count, tensor_size, col_width).transpose(1, 0, 2)
    target = (
        lax.psum_scatter(mixed, "tensor", scatter_dimension=0, tiled=True)
        .reshape(token_count, col_width)
        .astype(jnp.float32)
    )
    student_slot = slot_table(student_routes, DICTS, CAP_S)
    picked = student_slot[:, 0][:, None] == jnp.arange(DICTS * CAP_S, dtype=jnp.int32)[None, :]
    sending = picked.astype(jnp.bfloat16)
    selector = picked.astype(jnp.float32)
    outgoing = jnp.einsum("tc,tw->cw", sending, tokens, preferred_element_type=jnp.float32).astype(
        jnp.bfloat16
    )
    outgoing = jnp.repeat(outgoing.reshape(DICTS, CAP_S, col_width), span_size, axis=0)
    student_in = lax.all_to_all(outgoing, "expert", split_axis=0, concat_axis=0, tiled=True)
    sources = student_in.shape[0]
    rows = sources * CAP_S
    inputs_flat = student_in.reshape(rows, col_width)
    pre_part = jnp.dot(
        inputs_flat.astype(jnp.float32),
        enc_weight[0],
        precision=lax.Precision.HIGH,
        preferred_element_type=jnp.float32,
    )
    latent, pre_own = exchange(pre_part, enc_bias, False)
    partial_out = jnp.dot(
        latent.astype(jnp.float32),
        dec_weight[0],
        precision=lax.Precision.HIGH,
        preferred_element_type=jnp.float32,
    )
    back_parts = lax.all_to_all(
        partial_out.reshape(sources, CAP_S, col_width),
        "expert",
        split_axis=0,
        concat_axis=0,
        tiled=True,
    )
    estimate = jnp.sum(back_parts.reshape(DICTS, span_size, CAP_S, col_width), axis=1).reshape(
        DICTS * CAP_S, col_width
    )
    predicted = jnp.dot(
        selector, estimate, precision=lax.Precision.HIGHEST, preferred_element_type=jnp.float32
    )
    error_rows = (predicted - target) * error_scale
    error_slots = lax.dot_general(
        selector,
        error_rows,
        (((0,), (0,)), ((), ())),
        precision=lax.Precision.HIGHEST,
        preferred_element_type=jnp.float32,
    )
    error_slots = jnp.repeat(error_slots.reshape(DICTS, CAP_S, col_width), span_size, axis=0)
    error_back = lax.all_to_all(error_slots, "expert", split_axis=0, concat_axis=0, tiled=True)
    error_flat = error_back.reshape(rows, col_width)
    latent_part = lax.dot_general(
        error_flat,
        dec_weight[0],
        (((1,), (1,)), ((), ())),
        precision=lax.Precision.HIGH,
        preferred_element_type=jnp.float32,
    )
    dec_grad = lax.dot_general(
        latent,
        error_flat.astype(jnp.bfloat16),
        (((0,), (0,)), ((), ())),
        preferred_element_type=jnp.float32,
    )
    pre_grad = exchange(latent_part, pre_own, True)
    enc_grad = lax.dot_general(
        inputs_flat,
        pre_grad,
        (((0,), (0,)), ((), ())),
        preferred_element_type=jnp.float32,
    )
    bias_grad = jnp.sum(pre_grad.astype(jnp.float32), axis=0)
    return (enc_grad[None], bias_grad[None], dec_grad[None])


def solution(mesh):
    return jax.shard_map(
        on_device,
        mesh=mesh,
        in_specs=(
            P(("groups", "expert"), "tensor"),
            P(("groups", "expert"), None),
            P(("groups", "expert")),
            P(("groups", "expert"), None),
            P("expert", None, "tensor"),
            P("expert", None, "tensor"),
            P("expert", "tensor", None),
            P("expert", "tensor", None),
            P("expert", None),
            P("expert", None, "tensor"),
        ),
        out_specs=(
            P(("groups", "expert"), "tensor", None),
            P(("groups", "expert"), None),
            P(("groups", "expert"), None, "tensor"),
        ),
        check_vma=False,
    )
```

```python
import functools
import math

import jax
import jax.numpy as jnp
from jax import lax
from jax.experimental import pallas as pl
from jax.experimental.pallas import tpu as pltpu
from jax.sharding import PartitionSpec as P

EXPERTS = 4
DICTS = 4
CAP = 80
CAP_S = 48


error_scale = 0.0625


PIECES = 4
BLOCK = 16
ROOT = math.sqrt(2.0 / math.pi)
MESH_IDS = pl.DeviceIdType.MESH


def gelu_tail(v):
    return jnp.tanh(ROOT * (v + 0.044715 * (v * v * v)))


def exchange_kernel(
    n, backward, part_ref, aux_ref, out_ref, *rest
):
    if backward:
        own_ref = None
        send32, recv32, send16, recv16, s32, r32, s16, r16, sg, rg = rest
    else:
        own_ref, send32, recv32, send16, recv16, s32, r32, s16, r16, sg, rg = rest
    rows, cols = recv32.shape
    piece = rows // PIECES
    me = lax.axis_index("tensor")
    pair, bit = me // 2, me % 2
    partner = 2 * pair + 1 - bit
    others = []
    for q in range(1, n // 2):
        for c in range(2):
            others.append(2 * ((pair + q) % (n // 2)) + c)

    def columns(index):
        return pl.ds(pl.multiple_of(index * cols, cols), cols)

    barrier = pltpu.get_barrier_semaphore()
    for peer in [partner] + others:
        pl.semaphore_signal(barrier, inc=1, device_id={"tensor": peer}, device_id_type=MESH_IDS)
    pl.semaphore_wait(barrier, n - 1)

    sends = []
    for h in range(PIECES):
        span = pl.ds(h * piece, piece)
        for i, peer in enumerate(others):

            @pl.loop(0, piece // BLOCK)
            def _(j):
                r = pl.ds(pl.multiple_of(h * piece + j * BLOCK, BLOCK), BLOCK)
                send16[i, r, :] = part_ref[r, columns(peer)].astype(jnp.bfloat16)

            copy = pltpu.make_async_remote_copy(
                src_ref=send16.at[i, span],
                dst_ref=recv16.at[me, span],
                send_sem=s16.at[h, i],
                recv_sem=r16.at[h, me],
                device_id={"tensor": peer},
                device_id_type=MESH_IDS,
            )
            copy.start()
            sends.append(copy)

        @pl.loop(0, piece // BLOCK)
        def _(j):
            r = pl.ds(pl.multiple_of(h * piece + j * BLOCK, BLOCK), BLOCK)
            send32[r, :] = part_ref[r, columns(partner)]

        copy = pltpu.make_async_remote_copy(
            src_ref=send32.at[span],
            dst_ref=recv32.at[span],
            send_sem=s32.at[h],
            recv_sem=r32.at[h],
            device_id={"tensor": partner},
            device_id_type=MESH_IDS,
        )
        copy.start()
        sends.append(copy)

    def arrival(ref, sem, peer):
        return pltpu.make_async_remote_copy(
            src_ref=ref,
            dst_ref=ref,
            send_sem=sem,
            recv_sem=sem,
            device_id={"tensor": peer},
            device_id_type=MESH_IDS,
        )

    for h in range(PIECES):
        span = pl.ds(h * piece, piece)
        arrival(recv32.at[span], r32.at[h], partner).wait_recv()
        for peer in others:
            arrival(recv16.at[peer, span], r16.at[h, peer], peer).wait_recv()

        @pl.loop(0, piece // BLOCK)
        def _(j):
            r = pl.ds(pl.multiple_of(h * piece + j * BLOCK, BLOCK), BLOCK)
            total = part_ref[r, columns(me)] + recv32[r, :]
            for peer in others:
                total = total + recv16[peer, r, :].astype(jnp.float32)
            if backward:
                v = aux_ref[r, :]
                t = gelu_tail(v)
                slope = 0.5 * (1.0 + t) + (0.5 * ROOT) * v * (1.0 - t * t) * (
                    1.0 + (3.0 * 0.044715) * (v * v)
                )
                value = total * slope
            else:
                v = total + aux_ref[:, columns(me)]
                own_ref[r, :] = v
                value = 0.5 * v * (1.0 + gelu_tail(v))
            out_ref[r, columns(me)] = value.astype(jnp.bfloat16)

        for i, peer in enumerate([partner] + others):
            copy = pltpu.make_async_remote_copy(
                src_ref=out_ref.at[span, columns(me)],
                dst_ref=out_ref.at[span, columns(me)],
                send_sem=sg.at[h, i],
                recv_sem=rg.at[h, me],
                device_id={"tensor": peer},
                device_id_type=MESH_IDS,
            )
            copy.start()
            sends.append(copy)

    for h in range(PIECES):
        span = pl.ds(h * piece, piece)
        for peer in [partner] + others:
            arrival(out_ref.at[span, columns(peer)], rg.at[h, peer], peer).wait_recv()
    for copy in sends:
        copy.wait_send()


def exchange(part, aux, backward):
    n = lax.axis_size("tensor")
    rows, width = part.shape
    cols = width // n
    vmem = pl.BlockSpec(memory_space=pltpu.VMEM)
    gathered = jax.ShapeDtypeStruct((rows, width), jnp.bfloat16)
    own = jax.ShapeDtypeStruct((rows, cols), jnp.float32)
    dma = pltpu.SemaphoreType.DMA
    return pl.pallas_call(
        functools.partial(exchange_kernel, n, backward),
        out_shape=gathered if backward else (gathered, own),
        in_specs=[vmem, vmem],
        out_specs=vmem if backward else (vmem, vmem),
        scratch_shapes=[
            pltpu.VMEM((rows, cols), jnp.float32),
            pltpu.VMEM((rows, cols), jnp.float32),
            pltpu.VMEM((n - 2, rows, cols), jnp.bfloat16),
            pltpu.VMEM((n, rows, cols), jnp.bfloat16),
            dma((PIECES,)),
            dma((PIECES,)),
            dma((PIECES, n - 2)),
            dma((PIECES, n)),
            dma((PIECES, n - 1)),
            dma((PIECES, n)),
        ],
        compiler_params=pltpu.CompilerParams(
            collective_id=1 if backward else 0,
            has_side_effects=True,
            vmem_limit_bytes=32 * 1024 * 1024,
        ),
        cost_estimate=pl.CostEstimate(
            flops=20 * rows * cols, bytes_accessed=rows * width * 6, transcendentals=rows * cols
        ),
    )(part, aux)


def slot_table(routes, group_count, capacity):
    length, pick_count = routes.shape
    flat_ids = routes.reshape(length * pick_count)
    onehot = (flat_ids[:, None] == jnp.arange(group_count, dtype=jnp.int32)[None, :]).astype(
        jnp.int32
    )
    before = jnp.cumsum(onehot, axis=0) - onehot
    position = jnp.sum(before * onehot, axis=1)
    return (flat_ids * capacity + position).reshape(length, pick_count)


def on_device(
    tokens,
    teacher_routes,
    teacher_share,
    student_routes,
    gate_weight,
    up_weight,
    down_weight,
    enc_weight,
    enc_bias,
    dec_weight,
):
    span_size = lax.axis_size("expert") // EXPERTS
    col_width = tokens.shape[1]
    full_width = col_width * lax.axis_size("tensor")
    teacher_slot = slot_table(teacher_routes, EXPERTS, CAP)
    slot_hits = (
        teacher_slot[:, :, None] == jnp.arange(EXPERTS * CAP, dtype=jnp.int32)[None, None, :]
    )
    spread = jnp.any(slot_hits, axis=1).astype(jnp.bfloat16)
    shares = jnp.stack([teacher_share, 1.0 - teacher_share], axis=1)
    weighting = jnp.sum(jnp.where(slot_hits, shares[:, :, None], 0.0), axis=1)
    full_tokens = lax.all_gather(tokens, "tensor", axis=1, tiled=True)
    packed = jnp.einsum(
        "tc,tw->cw", spread, full_tokens, preferred_element_type=jnp.float32
    ).astype(jnp.bfloat16)
    packed = packed.reshape(EXPERTS, CAP, full_tokens.shape[1])
    arrived = lax.all_to_all(
        jnp.repeat(packed, span_size, axis=0), "expert", split_axis=0, concat_axis=0, tiled=True
    )
    sources, slot_count, _ = arrived.shape
    flat_rows = arrived.reshape(sources * slot_count, full_width)
    gate_proj = jnp.dot(flat_rows, gate_weight[0], preferred_element_type=jnp.float32)
    up_proj = jnp.dot(flat_rows, up_weight[0], preferred_element_type=jnp.float32)
    hidden = (jax.nn.silu(gate_proj) * up_proj).astype(jnp.bfloat16)
    part_rows = jnp.dot(hidden, down_weight[0], preferred_element_type=jnp.float32)
    part_rows = part_rows.astype(jnp.bfloat16).reshape(sources, slot_count, full_width)
    returned = lax.all_to_all(part_rows, "expert", split_axis=0, concat_axis=0, tiled=True)
    summed = jnp.sum(
        returned.astype(jnp.float32).reshape(EXPERTS, span_size, CAP, full_width), axis=1
    ).reshape(EXPERTS * CAP, full_width)
    mixed = jnp.dot(
        weighting, summed, precision=lax.Precision.HIGH, preferred_element_type=jnp.float32
    ).astype(jnp.bfloat16)
    tensor_size = lax.axis_size("tensor")
    token_count = mixed.shape[0]
    mixed = mixed.reshape(token_count, tensor_size, col_width).transpose(1, 0, 2)
    target = (
        lax.psum_scatter(mixed, "tensor", scatter_dimension=0, tiled=True)
        .reshape(token_count, col_width)
        .astype(jnp.float32)
    )
    student_slot = slot_table(student_routes, DICTS, CAP_S)
    picked = student_slot[:, 0][:, None] == jnp.arange(DICTS * CAP_S, dtype=jnp.int32)[None, :]
    sending = picked.astype(jnp.bfloat16)
    selector = picked.astype(jnp.float32)
    outgoing = jnp.einsum("tc,tw->cw", sending, tokens, preferred_element_type=jnp.float32).astype(
        jnp.bfloat16
    )
    outgoing = jnp.repeat(outgoing.reshape(DICTS, CAP_S, col_width), span_size, axis=0)
    student_in = lax.all_to_all(outgoing, "expert", split_axis=0, concat_axis=0, tiled=True)
    sources = student_in.shape[0]
    rows = sources * CAP_S
    inputs_flat = student_in.reshape(rows, col_width)
    pre_part = jnp.dot(
        inputs_flat.astype(jnp.float32),
        enc_weight[0],
        precision=lax.Precision.HIGH,
        preferred_element_type=jnp.float32,
    )
    lat_size = pre_part.shape[1]
    lat_cols = lat_size // tensor_size
    blocks = lax.optimization_barrier(pre_part).reshape(rows, tensor_size, lat_cols)
    pre_own = lax.psum_scatter(
        blocks.transpose(1, 0, 2), "tensor", scatter_dimension=0, tiled=True
    ).reshape(rows, lat_cols)
    bias_own = lax.dynamic_slice_in_dim(
        enc_bias[0], lax.axis_index("tensor") * lat_cols, lat_cols
    )
    pre_own = pre_own + bias_own[None, :]
    latent_own = 0.5 * pre_own * (1.0 + gelu_tail(pre_own))
    latent = (
        lax.all_gather(latent_own.astype(jnp.bfloat16), "tensor", axis=0, tiled=False)
        .transpose(1, 0, 2)
        .reshape(rows, lat_size)
    )
    partial_out = jnp.dot(
        latent.astype(jnp.float32),
        dec_weight[0],
        precision=lax.Precision.HIGH,
        preferred_element_type=jnp.float32,
    )
    back_parts = lax.all_to_all(
        partial_out.reshape(sources, CAP_S, col_width),
        "expert",
        split_axis=0,
        concat_axis=0,
        tiled=True,
    )
    estimate = jnp.sum(back_parts.reshape(DICTS, span_size, CAP_S, col_width), axis=1).reshape(
        DICTS * CAP_S, col_width
    )
    predicted = jnp.dot(
        selector, estimate, precision=lax.Precision.HIGHEST, preferred_element_type=jnp.float32
    )
    error_rows = (predicted - target) * error_scale
    error_slots = lax.dot_general(
        selector,
        error_rows,
        (((0,), (0,)), ((), ())),
        precision=lax.Precision.HIGHEST,
        preferred_element_type=jnp.float32,
    )
    error_slots = jnp.repeat(error_slots.reshape(DICTS, CAP_S, col_width), span_size, axis=0)
    error_back = lax.all_to_all(error_slots, "expert", split_axis=0, concat_axis=0, tiled=True)
    error_flat = error_back.reshape(rows, col_width)
    latent_part = lax.dot_general(
        error_flat,
        dec_weight[0],
        (((1,), (1,)), ((), ())),
        precision=lax.Precision.HIGH,
        preferred_element_type=jnp.float32,
    )
    dec_grad = lax.dot_general(
        latent,
        error_flat.astype(jnp.bfloat16),
        (((0,), (0,)), ((), ())),
        preferred_element_type=jnp.float32,
    )
    pre_grad = exchange(latent_part, pre_own, True)
    enc_grad = lax.dot_general(
        inputs_flat,
        pre_grad,
        (((0,), (0,)), ((), ())),
        preferred_element_type=jnp.float32,
    )
    bias_grad = jnp.sum(pre_grad.astype(jnp.float32), axis=0)
    return (enc_grad[None], bias_grad[None], dec_grad[None])


def solution(mesh):
    return jax.shard_map(
        on_device,
        mesh=mesh,
        in_specs=(
            P(("groups", "expert"), "tensor"),
            P(("groups", "expert"), None),
            P(("groups", "expert")),
            P(("groups", "expert"), None),
            P("expert", None, "tensor"),
            P("expert", None, "tensor"),
            P("expert", "tensor", None),
            P("expert", "tensor", None),
            P("expert", None),
            P("expert", None, "tensor"),
        ),
        out_specs=(
            P(("groups", "expert"), "tensor", None),
            P(("groups", "expert"), None),
            P(("groups", "expert"), None, "tensor"),
        ),
        check_vma=False,
    )
```
